32 devices in a mesh: stn: 8 (over z, y), sec: 4 (over x, core).
Axes of the slice: x: 2, y: 2, z: 4, core: 2. Of those that a mesh axis runs over, the one named last changes fastest.
Arguments:
- voltages: bfloat16 [2, 1024, 569344], P(None, ('stn', 'sec')), may hold values from -6 to 6
- fir_taps: float32 [12, 4096], replicated, may hold values from -1.75 to 1.75
- cor_channels: int32 [32], replicated, may hold values from 0 to 4095, as said below
- beam_channels: int32 [32], replicated, may hold values from 1 to 4094, as said below
- cor_gain: float32 [32], replicated, as said below
- beam_gain: float32 [32], replicated, as said below
- beam_stations: int32 [16, 512], replicated, may hold values from 0 to 511
- beam_codes: int32 [16, 512], replicated, may hold values from 0 to 255
Outputs:
- visibilities: bfloat16 [32, 2, 1024, 1024], P(('stn', 'sec'))
- beams: bfloat16 [32, 16, 2, 256], P(('stn', 'sec'))
The draws below stay inside these ranges and needn't reach their ends.
Inputs may be any that keep to these rules, and one draw needn't show every extreme that they name: cor_channels and beam_channels together are 64 distinct transform channels. None of beam_channels appears in cor_channels. `cor_gain`: positive. `beam_gain`: positive.
All inputs are finite; a program needn't handle non-finite values.
Results may differ from the reference program's by a relative error of at most 0.0085.
Values may be sent and summed in bfloat16 or wider, within the bound.
A program may use at most 320 MiB of HBM per device.

```python
import math
import jax
import jax.numpy as jnp
from jax import lax

STATIONS = 512
NFFT = 4096
TAPS = 12
NBEAM = 16
BEAM_STN = 512
SPECTRA = 128
INPUTS = 1024
FRAMES = 139
NCOR = 32
NBC = 32


def channel_lists(key):
    middle = (jax.random.permutation(jax.random.fold_in(key, 7), NFFT - 4) + 2).astype(jnp.int32)
    cor_ends = jnp.array([0, NFFT - 1], dtype=jnp.int32)
    beam_ends = jnp.array([1, NFFT - 2], dtype=jnp.int32)
    cor_list = jnp.concatenate([cor_ends, middle[:NCOR - 2]])
    beam_list = jnp.concatenate([beam_ends, middle[NCOR - 2:NCOR - 2 + NBC - 2]])
    cor_order = jax.random.permutation(jax.random.fold_in(key, 17), NCOR)
    beam_order = jax.random.permutation(jax.random.fold_in(key, 19), NBC)
    return (cor_list[cor_order].astype(jnp.int32), beam_list[beam_order].astype(jnp.int32))


def draw_cor_channels(key, part):
    return channel_lists(key)[0]


def draw_beam_channels(key, part):
    return channel_lists(key)[1]


def rising_gain(key, salt, length):
    position = jnp.arange(length, dtype=jnp.float32) / max(length - 1, 1)
    baseline = jnp.exp(position * math.log(3.0))
    subkey = jax.random.fold_in(key, salt)
    factor = jnp.exp(jax.random.uniform(subkey, (length,), jnp.float32, 0.0, math.log(3.3)))
    return baseline * factor


def draw_cor_gain(key, part):
    return rising_gain(key, 11, NCOR)


def draw_beam_gain(key, part):
    return rising_gain(key, 13, NBC)


def with_ends(result, stream_key, low, largest):
    place = [jax.random.randint(jax.random.fold_in(stream_key, axis), (), 0, length) for axis, length in enumerate(result.shape)]
    widest = result.shape.index(max(result.shape))
    neighbour = place[:widest] + [(place[widest] + 1) % result.shape[widest]] + place[widest + 1:]
    return result.at[tuple(place)].set(low).at[tuple(neighbour)].set(largest)


def steps_of(rng, dims, cuts, smallest, largest):
    def one(dim, shards_of):
        steps = jax.random.uniform(jax.random.fold_in(jax.random.fold_in(rng, 6), dim), (shards_of,), jnp.float32, smallest / len(cuts), largest / len(cuts))
        return jnp.repeat(jnp.exp(steps), dims[dim] // shards_of).reshape((-1,) + (1,) * (len(dims) - dim - 1))

    loudness = one(*cuts[0])
    for cut in cuts[1:]:
        loudness = loudness * one(*cut)
    return loudness


def normal_values(stream_key, dims, spread, reach, shards=(), kind=jnp.bfloat16):
    values = spread * jax.random.normal(stream_key, dims, jnp.float32)
    if shards:
        values = values * steps_of(stream_key, dims, shards, -0.22, 0.18)
    return jnp.clip(values, -reach, reach).astype(kind)


def setup_inputs(seed: int = 0) -> dict:
    arg_keys = jax.random.split(jax.random.key(seed), 9)
    return {
        "voltages": normal_values(arg_keys[0], (2, INPUTS, FRAMES * NFFT), 1.0, 6.0, ((1, 32),)),
        "fir_taps": normal_values(arg_keys[1], (TAPS, NFFT), TAPS ** -0.5, 1.75, (), jnp.float32),
        "cor_channels": draw_cor_channels(jax.random.fold_in(arg_keys[8], 71), 0),
        "beam_channels": draw_beam_channels(jax.random.fold_in(arg_keys[8], 71), 0),
        "cor_gain": draw_cor_gain(jax.random.fold_in(arg_keys[8], 71), 0),
        "beam_gain": draw_beam_gain(jax.random.fold_in(arg_keys[8], 71), 0),
        "beam_stations": with_ends(jax.random.randint(arg_keys[6], (NBEAM, BEAM_STN), 0, STATIONS), jax.random.fold_in(arg_keys[6], 1), 0, STATIONS - 1).astype(jnp.int32),
        "beam_codes": with_ends(jax.random.randint(arg_keys[7], (NBEAM, BEAM_STN), 0, 256), jax.random.fold_in(arg_keys[7], 1), 0, 255).astype(jnp.int32),
    }


epsilon = 1e-05

def make_tables(channel_of, points):
    sample_index = jnp.arange(points, dtype=jnp.int32)
    phase_turns = channel_of[:, None] * sample_index[None, :] % points
    phase_angle = phase_turns.astype(jnp.float32) * (2.0 * math.pi / points)
    table_scale = 1.0 / math.sqrt(points)
    cos_table = (jnp.cos(phase_angle) * table_scale).astype(jnp.bfloat16)
    sin_table = (jnp.sin(phase_angle) * table_scale).astype(jnp.bfloat16)
    return (cos_table, sin_table)

def make_weights(beam_stations, beam_codes, stations):
    station_ids = jnp.arange(stations, dtype=jnp.int32)
    onehot = (beam_stations[:, :, None] == station_ids[None, None, :]).astype(jnp.float32)
    amplitude = (1 + beam_codes // 64).astype(jnp.float32)
    phase_angle = (beam_codes % 64).astype(jnp.float32) * (2.0 * math.pi / 64.0)
    weight_re = jnp.einsum('bk,bks->bs', amplitude * jnp.cos(phase_angle), onehot)
    weight_im = jnp.einsum('bk,bks->bs', amplitude * jnp.sin(phase_angle), onehot)
    return (weight_re.astype(jnp.bfloat16), weight_im.astype(jnp.bfloat16))

def polyphase(in_block, fir_taps, spectra):
    tap_count, points = fir_taps.shape
    framed = in_block.reshape(in_block.shape[0], in_block.shape[1], -1, points)
    summed = jnp.zeros((framed.shape[0], framed.shape[1], spectra, points), jnp.float32)
    for tap_index in range(tap_count):
        summed = summed + fir_taps[tap_index] * framed[:, :, tap_index:tap_index + spectra, :].astype(jnp.float32)
    return summed.astype(jnp.bfloat16)

def spectrum(filtered, cos_table, sin_table, slot_gain):
    inputs_here, spectra, points = (filtered.shape[1], filtered.shape[2], filtered.shape[3])
    real_rows = filtered[0].reshape(inputs_here * spectra, points)
    imag_rows = filtered[1].reshape(inputs_here * spectra, points)
    spec_re = jnp.dot(cos_table, real_rows.T, preferred_element_type=jnp.float32) + jnp.dot(sin_table, imag_rows.T, preferred_element_type=jnp.float32)
    spec_im = jnp.dot(cos_table, imag_rows.T, preferred_element_type=jnp.float32) - jnp.dot(sin_table, real_rows.T, preferred_element_type=jnp.float32)
    combined = jnp.concatenate([spec_re.reshape(-1, inputs_here, spectra), spec_im.reshape(-1, inputs_here, spectra)], axis=2)
    return (combined * slot_gain[:, None, None]).astype(jnp.bfloat16)

def form_beams(beam_data, weight_re, weight_im):
    spectra = beam_data.shape[2] // 2
    samples = beam_data.astype(jnp.float32).reshape(beam_data.shape[0], -1, 2, beam_data.shape[2])
    with_re = jnp.einsum('bs,jspt->jbpt', weight_re.astype(jnp.float32), samples)
    with_im = jnp.einsum('bs,jspt->jbpt', weight_im.astype(jnp.float32), samples)
    out_re = with_re[..., :spectra] - with_im[..., spectra:]
    out_im = with_re[..., spectra:] + with_im[..., :spectra]
    return jnp.concatenate([out_re, out_im], axis=3)

def reference(voltages, fir_taps, cor_channels, beam_channels, cor_gain, beam_gain, beam_stations, beam_codes):
    channel_of = jnp.concatenate([cor_channels, beam_channels])
    slot_gain = jnp.concatenate([cor_gain, beam_gain])
    cos_table, sin_table = make_tables(channel_of, NFFT)
    block_inputs = 32
    block_count = INPUTS // block_inputs

    def one_block(block_index):
        first_input = (block_index * block_inputs).astype(jnp.int32)
        portion = lax.dynamic_slice_in_dim(voltages, first_input, block_inputs, 1)
        return spectrum(polyphase(portion, fir_taps, SPECTRA), cos_table, sin_table, slot_gain)
    blocked = lax.map(one_block, jnp.arange(block_count, dtype=jnp.int32))
    spectra = jnp.transpose(blocked, (1, 0, 2, 3)).reshape(NCOR + NBC, INPUTS, 2 * SPECTRA)

    def correlate(matrix):
        swapped = jnp.concatenate([matrix[:, SPECTRA:], -matrix[:, :SPECTRA]], axis=1)
        vis_re = jnp.dot(matrix, matrix.T, preferred_element_type=jnp.float32) / SPECTRA
        vis_im = jnp.dot(swapped, matrix.T, preferred_element_type=jnp.float32) / SPECTRA
        return jnp.stack([vis_re, vis_im]).astype(jnp.bfloat16)
    visibilities = lax.map(correlate, spectra[:NCOR])
    weight_re, weight_im = make_weights(beam_stations, beam_codes, STATIONS)
    raw_beams = form_beams(spectra[NCOR:], weight_re, weight_im)
    entry_count = raw_beams.shape[0] * raw_beams.shape[2] * raw_beams.shape[3]
    beam_power = lax.optimization_barrier(jnp.sum(raw_beams * raw_beams, axis=(0, 2, 3))) / entry_count
    beams = (raw_beams * lax.rsqrt(beam_power + epsilon)[None, :, None, None]).astype(jnp.bfloat16)
    return (visibilities, beams)
```

```python
import functools
import math

import jax
import jax.numpy as jnp
from jax import lax
from jax.experimental import pallas as pl
from jax.experimental.pallas import tpu as pltpu
from jax.sharding import PartitionSpec as P

STATIONS = 512


epsilon = 1e-05


def make_tables(channel_of, points):
    sample_index = jnp.arange(points, dtype=jnp.int32)
    phase_turns = channel_of[:, None] * sample_index[None, :] % points
    phase_angle = phase_turns.astype(jnp.float32) * (2.0 * math.pi / points)
    table_scale = 1.0 / math.sqrt(points)
    cos_table = (jnp.cos(phase_angle) * table_scale).astype(jnp.bfloat16)
    sin_table = (jnp.sin(phase_angle) * table_scale).astype(jnp.bfloat16)
    return (cos_table, sin_table)


def make_weights(beam_stations, beam_codes, stations):
    station_ids = jnp.arange(stations, dtype=jnp.int32)
    onehot = (beam_stations[:, :, None] == station_ids[None, None, :]).astype(jnp.float32)
    amplitude = (1 + beam_codes // 64).astype(jnp.float32)
    phase_angle = (beam_codes % 64).astype(jnp.float32) * (2.0 * math.pi / 64.0)
    weight_re = jnp.einsum("bk,bks->bs", amplitude * jnp.cos(phase_angle), onehot)
    weight_im = jnp.einsum("bk,bks->bs", amplitude * jnp.sin(phase_angle), onehot)
    return (weight_re.astype(jnp.bfloat16), weight_im.astype(jnp.bfloat16))


def polyphase(in_block, fir_taps, spectra):
    tap_count, points = fir_taps.shape
    framed = in_block.reshape(in_block.shape[0], in_block.shape[1], -1, points)
    summed = jnp.zeros((framed.shape[0], framed.shape[1], spectra, points), jnp.float32)
    for tap_index in range(tap_count):
        summed = summed + fir_taps[tap_index] * framed[
            :, :, tap_index : tap_index + spectra, :
        ].astype(jnp.float32)
    return summed.astype(jnp.bfloat16)


def contract(left_rows, right_rows):
    contract_dims = (((1,), (1,)), ((), ()))
    return lax.dot_general(left_rows, right_rows, contract_dims, preferred_element_type=jnp.float32)


def spectrum(filtered, cos_table, sin_table, slot_gain):
    inputs_here, spectra, points = (filtered.shape[1], filtered.shape[2], filtered.shape[3])
    real_rows = filtered[0].reshape(inputs_here * spectra, points)
    imag_rows = filtered[1].reshape(inputs_here * spectra, points)
    spec_re = contract(cos_table, real_rows) + contract(sin_table, imag_rows)
    spec_im = contract(cos_table, imag_rows) - contract(sin_table, real_rows)
    combined = jnp.concatenate(
        [spec_re.reshape(-1, inputs_here, spectra), spec_im.reshape(-1, inputs_here, spectra)],
        axis=2,
    )
    return (combined * slot_gain[:, None, None]).astype(jnp.bfloat16)


def form_beams(beam_data, weight_re, weight_im):
    spectra = beam_data.shape[2] // 2
    samples = beam_data.reshape(beam_data.shape[0], -1, 2, beam_data.shape[2])
    with_re = jnp.einsum("bs,jspt->jbpt", weight_re, samples, preferred_element_type=jnp.float32)
    with_im = jnp.einsum("bs,jspt->jbpt", weight_im, samples, preferred_element_type=jnp.float32)
    out_re = with_re[..., :spectra] - with_im[..., spectra:]
    out_im = with_re[..., spectra:] + with_im[..., :spectra]
    return jnp.concatenate([out_re, out_im], axis=3)


def plain_device(
    voltages, fir_taps, cor_channels, beam_channels, cor_gain, beam_gain, beam_stations, beam_codes
):
    tap_count, points = fir_taps.shape
    stn_count = lax.axis_size("stn")
    sec_count = lax.axis_size("sec")
    device_count = stn_count * sec_count
    inputs_here = voltages.shape[1]
    spectra = voltages.shape[2] // points - tap_count + 1
    filtered = polyphase(voltages, fir_taps, spectra)
    channel_of = jnp.concatenate([cor_channels, beam_channels])
    slot_gain = jnp.concatenate([cor_gain, beam_gain])
    cos_table, sin_table = make_tables(channel_of, points)
    weight_re, weight_im = make_weights(beam_stations, beam_codes, STATIONS)
    spectra_all = spectrum(filtered, cos_table, sin_table, slot_gain)
    outgoing = spectra_all.reshape(2, stn_count, sec_count, 1, 1, inputs_here, 2 * spectra)
    turned = lax.all_to_all(
        lax.all_to_all(outgoing, "stn", split_axis=1, concat_axis=3, tiled=True),
        "sec",
        split_axis=2,
        concat_axis=4,
        tiled=True,
    )
    received = turned.reshape(2, device_count * inputs_here, 2 * spectra)
    cor_data = received[0]
    beam_data = received[1:2]
    swapped = jnp.concatenate([cor_data[:, spectra:], -cor_data[:, :spectra]], axis=1)
    vis_re = contract(cor_data, cor_data) / spectra
    vis_im = contract(swapped, cor_data) / spectra
    visibilities = jnp.stack([vis_re, vis_im])[None].astype(jnp.bfloat16)
    raw_beams = form_beams(beam_data, weight_re, weight_im)
    local_power = jnp.sum(raw_beams * raw_beams, axis=(0, 2, 3))
    summed_power = lax.psum(local_power, ("stn", "sec"))
    beam_power = summed_power / (device_count * raw_beams.shape[2] * raw_beams.shape[3])
    beams = (raw_beams * lax.rsqrt(beam_power + epsilon)[None, :, None, None]).astype(jnp.bfloat16)
    return (visibilities, beams)


MESH = pl.DeviceIdType.MESH
ROWS = 16
CHUNK = 512
STEP = 256


def split_tables(channel_of, points):
    coarse = 1 << (int(math.log2(points)) // 2)
    index = jnp.arange(coarse, dtype=jnp.int32)
    other = jnp.arange(points // coarse, dtype=jnp.int32)

    def pair(turns):
        angle = (turns % points).astype(jnp.float32) * (2.0 * math.pi / points)
        return jnp.cos(angle), jnp.sin(angle)

    high_cos, high_sin = pair(other[:, None] * coarse * channel_of[None, :])
    low_cos, low_sin = pair(index[:, None] * channel_of[None, :])
    high_cos, high_sin = high_cos[:, None, :], high_sin[:, None, :]
    low_cos, low_sin = low_cos[None], low_sin[None]
    scale = 1.0 / math.sqrt(points)
    cosine = ((high_cos * low_cos - high_sin * low_sin) * scale).astype(jnp.bfloat16)
    sine = ((high_sin * low_cos + high_cos * low_sin) * scale).astype(jnp.bfloat16)
    cosine = cosine.reshape(points, -1)
    sine = sine.reshape(points, -1)
    return jnp.stack(
        [jnp.concatenate([cosine, -sine], axis=1), jnp.concatenate([sine, cosine], axis=1)]
    )


def tree_sum(terms):
    while len(terms) > 1:
        paired = [terms[k] + terms[k + 1] for k in range(0, len(terms) - 1, 2)]
        if len(terms) % 2:
            paired.append(terms[-1])
        terms = paired
    return terms[0]


def channelize_kernel(
    points, tap_count, frames, groups, volt_ref, taps_ref, table_ref, gain_ref, out_ref,
    held, filtered, total, sem,
):
    chunks = points // CHUNK
    spectra = frames - tap_count + 1
    slots = gain_ref.shape[1] // 2
    group, chunk = pl.program_id(0), pl.program_id(1)
    step = group * chunks + chunk

    def fetch(which, slot):
        rows = pl.ds(pl.multiple_of((which // chunks) * ROWS, ROWS), ROWS)
        start = (which % chunks) * CHUNK

        def one(frame, carry):
            lanes = pl.ds(pl.multiple_of(frame * points + start, CHUNK), CHUNK)
            pltpu.make_async_copy(
                volt_ref.at[:, rows, lanes], held.at[slot, frame], sem.at[slot]
            ).start()
            return carry

        lax.fori_loop(0, frames, one, 0)

    slot = step % 2

    @pl.when(step == 0)
    def _():
        fetch(step, 0)

    @pl.when(step + 1 < groups * chunks)
    def _():
        fetch(step + 1, 1 - slot)

    pltpu.make_async_copy(held.at[slot], held.at[slot], sem.at[slot]).wait()

    @pl.when(chunk == 0)
    def _():
        total[...] = jnp.zeros_like(total)

    def unit(index, carry):
        part, piece = index // (CHUNK // STEP), index % (CHUNK // STEP)
        for tile in range(STEP // 128):
            here = pl.multiple_of(piece * STEP + tile * 128, 128)
            lanes = pl.ds(here, 128)
            point = pl.ds(pl.multiple_of(chunk * CHUNK + here, 128), 128)
            taps = [taps_ref[t, :, point] for t in range(tap_count)]
            window = [held[slot, t, part, :, lanes] for t in range(tap_count - 1)]
            for s in range(spectra):
                window.append(held[slot, s + tap_count - 1, part, :, lanes])
                value = tree_sum([tap * frame for tap, frame in zip(taps, window)])
                filtered[s * ROWS : (s + 1) * ROWS, tile * 128 : (tile + 1) * 128] = value
                window = window[1:]
        span = pl.ds(pl.multiple_of(chunk * CHUNK + piece * STEP, STEP), STEP)
        total[...] += jnp.dot(
            filtered[...], table_ref[part, span, :], preferred_element_type=jnp.float32
        )
        return carry

    lax.fori_loop(0, 2 * (CHUNK // STEP), unit, 0)

    @pl.when(chunk == chunks - 1)
    def _():
        for row in range(ROWS):
            mine = total[pl.ds(row, spectra, stride=ROWS), :] * gain_ref[...]
            turned = mine.T.astype(jnp.bfloat16)
            at = row * 2 * spectra
            out_ref[:, at : at + spectra] = turned[:slots]
            out_ref[:, at + spectra : at + 2 * spectra] = turned[slots:]


def channelize(voltages, fir_taps, table, slot_gain):
    tap_count, points = fir_taps.shape
    inputs_here = voltages.shape[1]
    frames = voltages.shape[2] // points
    spectra = frames - tap_count + 1
    slots = slot_gain.shape[0]
    groups = inputs_here // ROWS
    taps = jnp.broadcast_to(fir_taps.astype(jnp.bfloat16)[:, None, :], (tap_count, ROWS, points))
    gain = jnp.concatenate([slot_gain, slot_gain])[None, :]
    whole = pl.BlockSpec(memory_space=pltpu.VMEM)
    width = ROWS * 2 * spectra
    return pl.pallas_call(
        functools.partial(channelize_kernel, points, tap_count, frames, groups),
        grid=(groups, points // CHUNK),
        out_shape=jax.ShapeDtypeStruct((slots, inputs_here * 2 * spectra), jnp.bfloat16),
        in_specs=[pl.BlockSpec(memory_space=pl.ANY), whole, whole, whole],
        out_specs=pl.BlockSpec((slots, width), lambda group, chunk: (0, group)),
        scratch_shapes=[
            pltpu.VMEM((2, frames, 2, ROWS, CHUNK), jnp.bfloat16),
            pltpu.VMEM((spectra * ROWS, STEP), jnp.bfloat16),
            pltpu.VMEM((spectra * ROWS, 2 * slots), jnp.float32),
            pltpu.SemaphoreType.DMA((2,)),
        ],
        compiler_params=pltpu.CompilerParams(
            dimension_semantics=("arbitrary", "arbitrary"), vmem_limit_bytes=48 * 1024 * 1024
        ),
        name="channelize",
    )(voltages, taps, table, gain)


def place_of(index, sec_count):
    return (index // sec_count, lax.rem(index, sec_count))


def greet_all(me, count, sec_count):
    barrier = pltpu.get_barrier_semaphore()

    def greet(k, carry):
        pl.semaphore_signal(
            barrier, inc=1, device_id=place_of(lax.rem(me + k, count), sec_count),
            device_id_type=MESH,
        )
        return carry

    lax.fori_loop(1, count, greet, 0)
    pl.semaphore_wait(barrier, count - 1)


def exchange_kernel(count, sec_count, x_ref, y_ref, send_sem, recv_sem, own_sem):
    me = lax.axis_index("stn") * sec_count + lax.axis_index("sec")
    own = pltpu.make_async_copy(x_ref.at[:, me], y_ref.at[:, me], own_sem)
    own.start()
    greet_all(me, count, sec_count)

    def copy(k):
        to = lax.rem(me + k, count)
        return pltpu.make_async_remote_copy(
            src_ref=x_ref.at[:, to],
            dst_ref=y_ref.at[:, me],
            send_sem=send_sem.at[k],
            recv_sem=recv_sem.at[k],
            device_id=place_of(to, sec_count),
            device_id_type=MESH,
        )

    def start(k, carry):
        copy(k).start()
        return carry

    def finish(k, carry):
        copy(k).wait()
        return carry

    lax.fori_loop(1, count, start, 0)
    lax.fori_loop(1, count, finish, 0)
    own.wait()


def exchange(x, count, sec_count):
    return pl.pallas_call(
        functools.partial(exchange_kernel, count, sec_count),
        out_shape=jax.ShapeDtypeStruct(x.shape, x.dtype),
        in_specs=[pl.BlockSpec(memory_space=pl.ANY)],
        out_specs=pl.BlockSpec(memory_space=pl.ANY),
        scratch_shapes=[
            pltpu.SemaphoreType.DMA((count,)),
            pltpu.SemaphoreType.DMA((count,)),
            pltpu.SemaphoreType.DMA,
        ],
        compiler_params=pltpu.CompilerParams(collective_id=0, has_side_effects=True),
        name="exchange",
    )(x)


def power_kernel(count, sec_count, x_ref, y_ref, slots, send_sem, recv_sem):
    me = lax.axis_index("stn") * sec_count + lax.axis_index("sec")
    greet_all(me, count, sec_count)

    def copy(k):
        return pltpu.make_async_remote_copy(
            src_ref=x_ref,
            dst_ref=slots.at[k],
            send_sem=send_sem.at[k],
            recv_sem=recv_sem.at[k],
            device_id=place_of(lax.rem(me + k, count), sec_count),
            device_id_type=MESH,
        )

    def start(k, carry):
        copy(k).start()
        return carry

    def finish(k, carry):
        copy(k).wait()
        return carry

    lax.fori_loop(1, count, start, 0)
    slots[0] = x_ref[...]
    lax.fori_loop(1, count, finish, 0)
    y_ref[...] = jnp.sum(slots[...], axis=0)


def total_power(local_power, count, sec_count):
    beams = local_power.shape[0]
    x = jnp.broadcast_to(local_power[:, None], (beams, 128))
    summed = pl.pallas_call(
        functools.partial(power_kernel, count, sec_count),
        out_shape=jax.ShapeDtypeStruct(x.shape, x.dtype),
        in_specs=[pl.BlockSpec(memory_space=pltpu.VMEM)],
        out_specs=pl.BlockSpec(memory_space=pltpu.VMEM),
        scratch_shapes=[
            pltpu.VMEM((count,) + x.shape, x.dtype),
            pltpu.SemaphoreType.DMA((count,)),
            pltpu.SemaphoreType.DMA((count,)),
        ],
        compiler_params=pltpu.CompilerParams(collective_id=1, has_side_effects=True),
        name="power",
    )(x)
    return summed[:, 0]


def per_device(
    voltages, fir_taps, cor_channels, beam_channels, cor_gain, beam_gain, beam_stations, beam_codes
):
    tap_count, points = fir_taps.shape
    sec_count = lax.axis_size("sec")
    device_count = lax.axis_size("stn") * sec_count
    inputs_here = voltages.shape[1]
    frames = voltages.shape[2] // points
    spectra = frames - tap_count + 1
    slots = 2 * cor_channels.shape[0]
    fits = inputs_here % ROWS == 0 and points % CHUNK == 0 and spectra % 128 == 0
    if not fits or slots != 2 * device_count or slots % 16:
        return plain_device(
            voltages, fir_taps, cor_channels, beam_channels, cor_gain, beam_gain,
            beam_stations, beam_codes,
        )
    channel_of = jnp.concatenate([cor_channels, beam_channels])
    slot_gain = jnp.concatenate([cor_gain, beam_gain])
    table = split_tables(channel_of, points)
    weight_re, weight_im = make_weights(beam_stations, beam_codes, STATIONS)
    outgoing = channelize(voltages, fir_taps, table, slot_gain)
    outgoing = outgoing.reshape(2, device_count, inputs_here, 2 * spectra)
    received = exchange(outgoing, device_count, sec_count)
    received = received.reshape(2, device_count * inputs_here, 2 * spectra)
    cor_data = received[0]
    beam_data = received[1:2]
    raw_beams = form_beams(beam_data, weight_re, weight_im)
    local_power = jnp.sum(raw_beams * raw_beams, axis=(0, 2, 3))
    summed_power = total_power(local_power, device_count, sec_count)
    swapped = jnp.concatenate([cor_data[:, spectra:], -cor_data[:, :spectra]], axis=1)
    vis_re = contract(cor_data, cor_data) / spectra
    vis_im = contract(swapped, cor_data) / spectra
    visibilities = jnp.stack([vis_re, vis_im])[None].astype(jnp.bfloat16)
    beam_power = summed_power / (device_count * raw_beams.shape[2] * raw_beams.shape[3])
    beams = (raw_beams * lax.rsqrt(beam_power + epsilon)[None, :, None, None]).astype(jnp.bfloat16)
    return (visibilities, beams)


def solution(mesh):
    in_specs = (P(None, ("stn", "sec"), None), P(), P(), P(), P(), P(), P(), P())
    out_specs = (P(("stn", "sec"), None, None, None), P(("stn", "sec"), None, None, None))
    return jax.shard_map(
        per_device, mesh=mesh, in_specs=in_specs, out_specs=out_specs, check_vma=False
    )
```

```python
import functools
import math

import jax
import jax.numpy as jnp
from jax import lax
from jax.experimental import pallas as pl
from jax.experimental.pallas import tpu as pltpu
from jax.sharding import PartitionSpec as P

STATIONS = 512


epsilon = 1e-05


def make_tables(channel_of, points):
    sample_index = jnp.arange(points, dtype=jnp.int32)
    phase_turns = channel_of[:, None] * sample_index[None, :] % points
    phase_angle = phase_turns.astype(jnp.float32) * (2.0 * math.pi / points)
    table_scale = 1.0 / math.sqrt(points)
    cos_table = (jnp.cos(phase_angle) * table_scale).astype(jnp.bfloat16)
    sin_table = (jnp.sin(phase_angle) * table_scale).astype(jnp.bfloat16)
    return (cos_table, sin_table)


def make_weights(beam_stations, beam_codes, stations):
    station_ids = jnp.arange(stations, dtype=jnp.int32)
    onehot = (beam_stations[:, :, None] == station_ids[None, None, :]).astype(jnp.float32)
    amplitude = (1 + beam_codes // 64).astype(jnp.float32)
    phase_angle = (beam_codes % 64).astype(jnp.float32) * (2.0 * math.pi / 64.0)
    weight_re = jnp.einsum("bk,bks->bs", amplitude * jnp.cos(phase_angle), onehot)
    weight_im = jnp.einsum("bk,bks->bs", amplitude * jnp.sin(phase_angle), onehot)
    return (weight_re.astype(jnp.bfloat16), weight_im.astype(jnp.bfloat16))


def polyphase(in_block, fir_taps, spectra):
    tap_count, points = fir_taps.shape
    framed = in_block.reshape(in_block.shape[0], in_block.shape[1], -1, points)
    summed = jnp.zeros((framed.shape[0], framed.shape[1], spectra, points), jnp.float32)
    for tap_index in range(tap_count):
        summed = summed + fir_taps[tap_index] * framed[
            :, :, tap_index : tap_index + spectra, :
        ].astype(jnp.float32)
    return summed.astype(jnp.bfloat16)


def contract(left_rows, right_rows):
    contract_dims = (((1,), (1,)), ((), ()))
    return lax.dot_general(left_rows, right_rows, contract_dims, preferred_element_type=jnp.float32)


def spectrum(filtered, cos_table, sin_table, slot_gain):
    inputs_here, spectra, points = (filtered.shape[1], filtered.shape[2], filtered.shape[3])
    real_rows = filtered[0].reshape(inputs_here * spectra, points)
    imag_rows = filtered[1].reshape(inputs_here * spectra, points)
    spec_re = contract(cos_table, real_rows) + contract(sin_table, imag_rows)
    spec_im = contract(cos_table, imag_rows) - contract(sin_table, real_rows)
    combined = jnp.concatenate(
        [spec_re.reshape(-1, inputs_here, spectra), spec_im.reshape(-1, inputs_here, spectra)],
        axis=2,
    )
    return (combined * slot_gain[:, None, None]).astype(jnp.bfloat16)


def form_beams(beam_data, weight_re, weight_im):
    spectra = beam_data.shape[2] // 2
    samples = beam_data.reshape(beam_data.shape[0], -1, 2, beam_data.shape[2])
    with_re = jnp.einsum("bs,jspt->jbpt", weight_re, samples, preferred_element_type=jnp.float32)
    with_im = jnp.einsum("bs,jspt->jbpt", weight_im, samples, preferred_element_type=jnp.float32)
    out_re = with_re[..., :spectra] - with_im[..., spectra:]
    out_im = with_re[..., spectra:] + with_im[..., :spectra]
    return jnp.concatenate([out_re, out_im], axis=3)


def plain_device(
    voltages, fir_taps, cor_channels, beam_channels, cor_gain, beam_gain, beam_stations, beam_codes
):
    tap_count, points = fir_taps.shape
    stn_count = lax.axis_size("stn")
    sec_count = lax.axis_size("sec")
    device_count = stn_count * sec_count
    inputs_here = voltages.shape[1]
    spectra = voltages.shape[2] // points - tap_count + 1
    filtered = polyphase(voltages, fir_taps, spectra)
    channel_of = jnp.concatenate([cor_channels, beam_channels])
    slot_gain = jnp.concatenate([cor_gain, beam_gain])
    cos_table, sin_table = make_tables(channel_of, points)
    weight_re, weight_im = make_weights(beam_stations, beam_codes, STATIONS)
    spectra_all = spectrum(filtered, cos_table, sin_table, slot_gain)
    outgoing = spectra_all.reshape(2, stn_count, sec_count, 1, 1, inputs_here, 2 * spectra)
    turned = lax.all_to_all(
        lax.all_to_all(outgoing, "stn", split_axis=1, concat_axis=3, tiled=True),
        "sec",
        split_axis=2,
        concat_axis=4,
        tiled=True,
    )
    received = turned.reshape(2, device_count * inputs_here, 2 * spectra)
    cor_data = received[0]
    beam_data = received[1:2]
    swapped = jnp.concatenate([cor_data[:, spectra:], -cor_data[:, :spectra]], axis=1)
    vis_re = contract(cor_data, cor_data) / spectra
    vis_im = contract(swapped, cor_data) / spectra
    visibilities = jnp.stack([vis_re, vis_im])[None].astype(jnp.bfloat16)
    raw_beams = form_beams(beam_data, weight_re, weight_im)
    local_power = jnp.sum(raw_beams * raw_beams, axis=(0, 2, 3))
    summed_power = lax.psum(local_power, ("stn", "sec"))
    beam_power = summed_power / (device_count * raw_beams.shape[2] * raw_beams.shape[3])
    beams = (raw_beams * lax.rsqrt(beam_power + epsilon)[None, :, None, None]).astype(jnp.bfloat16)
    return (visibilities, beams)


MESH = pl.DeviceIdType.MESH
ROWS = 16
CHUNK = 1024
STEP = 256


def split_tables(channel_of, points):
    coarse = 1 << (int(math.log2(points)) // 2)
    index = jnp.arange(coarse, dtype=jnp.int32)
    other = jnp.arange(points // coarse, dtype=jnp.int32)

    def pair(turns):
        angle = (turns % points).astype(jnp.float32) * (2.0 * math.pi / points)
        return jnp.cos(angle), jnp.sin(angle)

    high_cos, high_sin = pair(other[:, None] * coarse * channel_of[None, :])
    low_cos, low_sin = pair(index[:, None] * channel_of[None, :])
    high_cos, high_sin = high_cos[:, None, :], high_sin[:, None, :]
    low_cos, low_sin = low_cos[None], low_sin[None]
    scale = 1.0 / math.sqrt(points)
    cosine = ((high_cos * low_cos - high_sin * low_sin) * scale).astype(jnp.bfloat16)
    sine = ((high_sin * low_cos + high_cos * low_sin) * scale).astype(jnp.bfloat16)
    cosine = cosine.reshape(points, -1)
    sine = sine.reshape(points, -1)
    return jnp.stack(
        [jnp.concatenate([cosine, -sine], axis=1), jnp.concatenate([sine, cosine], axis=1)]
    )


def channelize_kernel(
    points, tap_count, frames, groups, volt_ref, taps_ref, table_ref, gain_ref, out_ref,
    held, filtered, total, sem,
):
    chunks = points // CHUNK
    spectra = frames - tap_count + 1
    slots = gain_ref.shape[1] // 2
    group, chunk = pl.program_id(0), pl.program_id(1)
    step = group * chunks + chunk

    def fetch(which, slot):
        rows = pl.ds(pl.multiple_of((which // chunks) * ROWS, ROWS), ROWS)
        start = (which % chunks) * CHUNK

        def one(frame, carry):
            lanes = pl.ds(pl.multiple_of(frame * points + start, CHUNK), CHUNK)
            pltpu.make_async_copy(
                volt_ref.at[:, rows, lanes], held.at[slot, frame], sem.at[slot]
            ).start()
            return carry

        lax.fori_loop(0, frames, one, 0)

    slot = step % 2

    @pl.when(step == 0)
    def _():
        fetch(step, 0)

    @pl.when(step + 1 < groups * chunks)
    def _():
        fetch(step + 1, 1 - slot)

    pltpu.make_async_copy(held.at[slot], held.at[slot], sem.at[slot]).wait()

    @pl.when(chunk == 0)
    def _():
        total[...] = jnp.zeros_like(total)

    def unit(index, carry):
        part, piece = index // (CHUNK // STEP), index % (CHUNK // STEP)
        for tile in range(STEP // 128):
            here = pl.multiple_of(piece * STEP + tile * 128, 128)
            lanes = pl.ds(here, 128)
            point = pl.ds(pl.multiple_of(chunk * CHUNK + here, 128), 128)
            taps = [taps_ref[t, :, point] for t in range(tap_count)]

            def load(frame):
                wide = held[slot, frame, part, :, lanes].astype(jnp.float32)
                return wide[:8], wide[8:]

            window = [load(t) for t in range(tap_count - 1)]
            for s in range(spectra):
                window.append(load(s + tap_count - 1))
                halves = []
                for half in range(2):
                    value = taps[0] * window[0][half]
                    for t in range(1, tap_count):
                        value = value + taps[t] * window[t][half]
                    halves.append(value)
                value = jnp.concatenate(halves, axis=0).astype(jnp.bfloat16)
                filtered[s * ROWS : (s + 1) * ROWS, tile * 128 : (tile + 1) * 128] = value
                window = window[1:]
        span = pl.ds(pl.multiple_of(chunk * CHUNK + piece * STEP, STEP), STEP)
        total[...] += jnp.dot(
            filtered[...], table_ref[part, span, :], preferred_element_type=jnp.float32
        )
        return carry

    lax.fori_loop(0, 2 * (CHUNK // STEP), unit, 0)

    @pl.when(chunk == chunks - 1)
    def _():
        for row in range(ROWS):
            mine = total[pl.ds(row, spectra, stride=ROWS), :] * gain_ref[...]
            turned = mine.T.astype(jnp.bfloat16)
            at = row * 2 * spectra
            out_ref[:, at : at + spectra] = turned[:slots]
            out_ref[:, at + spectra : at + 2 * spectra] = turned[slots:]


def channelize(voltages, fir_taps, table, slot_gain):
    tap_count, points = fir_taps.shape
    inputs_here = voltages.shape[1]
    frames = voltages.shape[2] // points
    spectra = frames - tap_count + 1
    slots = slot_gain.shape[0]
    groups = inputs_here // ROWS
    taps = jnp.broadcast_to(fir_taps[:, None, :], (tap_count, 8, points))
    gain = jnp.concatenate([slot_gain, slot_gain])[None, :]
    whole = pl.BlockSpec(memory_space=pltpu.VMEM)
    width = ROWS * 2 * spectra
    return pl.pallas_call(
        functools.partial(channelize_kernel, points, tap_count, frames, groups),
        grid=(groups, points // CHUNK),
        out_shape=jax.ShapeDtypeStruct((slots, inputs_here * 2 * spectra), jnp.bfloat16),
        in_specs=[pl.BlockSpec(memory_space=pl.ANY), whole, whole, whole],
        out_specs=pl.BlockSpec((slots, width), lambda group, chunk: (0, group)),
        scratch_shapes=[
            pltpu.VMEM((2, frames, 2, ROWS, CHUNK), jnp.bfloat16),
            pltpu.VMEM((spectra * ROWS, STEP), jnp.bfloat16),
            pltpu.VMEM((spectra * ROWS, 2 * slots), jnp.float32),
            pltpu.SemaphoreType.DMA((2,)),
        ],
        compiler_params=pltpu.CompilerParams(
            dimension_semantics=("arbitrary", "arbitrary"), vmem_limit_bytes=48 * 1024 * 1024
        ),
        name="channelize",
    )(voltages, taps, table, gain)


def place_of(index, sec_count):
    return (index // sec_count, lax.rem(index, sec_count))


def greet_all(me, count, sec_count):
    barrier = pltpu.get_barrier_semaphore()

    def greet(k, carry):
        pl.semaphore_signal(
            barrier, inc=1, device_id=place_of(lax.rem(me + k, count), sec_count),
            device_id_type=MESH,
        )
        return carry

    lax.fori_loop(1, count, greet, 0)
    pl.semaphore_wait(barrier, count - 1)


def exchange_kernel(count, sec_count, x_ref, y_ref, send_sem, recv_sem, own_sem):
    me = lax.axis_index("stn") * sec_count + lax.axis_index("sec")
    own = pltpu.make_async_copy(x_ref.at[:, me], y_ref.at[:, me], own_sem)
    own.start()
    greet_all(me, count, sec_count)

    def copy(k):
        to = lax.rem(me + k, count)
        return pltpu.make_async_remote_copy(
            src_ref=x_ref.at[:, to],
            dst_ref=y_ref.at[:, me],
            send_sem=send_sem.at[k],
            recv_sem=recv_sem.at[k],
            device_id=place_of(to, sec_count),
            device_id_type=MESH,
        )

    def start(k, carry):
        copy(k).start()
        return carry

    def finish(k, carry):
        copy(k).wait()
        return carry

    lax.fori_loop(1, count, start, 0)
    lax.fori_loop(1, count, finish, 0)
    own.wait()


def exchange(x, count, sec_count):
    return pl.pallas_call(
        functools.partial(exchange_kernel, count, sec_count),
        out_shape=jax.ShapeDtypeStruct(x.shape, x.dtype),
        in_specs=[pl.BlockSpec(memory_space=pl.ANY)],
        out_specs=pl.BlockSpec(memory_space=pl.ANY),
        scratch_shapes=[
            pltpu.SemaphoreType.DMA((count,)),
            pltpu.SemaphoreType.DMA((count,)),
            pltpu.SemaphoreType.DMA,
        ],
        compiler_params=pltpu.CompilerParams(collective_id=0, has_side_effects=True),
        name="exchange",
    )(x)


def power_kernel(count, sec_count, x_ref, y_ref, slots, send_sem, recv_sem):
    me = lax.axis_index("stn") * sec_count + lax.axis_index("sec")
    greet_all(me, count, sec_count)

    def copy(k):
        return pltpu.make_async_remote_copy(
            src_ref=x_ref,
            dst_ref=slots.at[k],
            send_sem=send_sem.at[k],
            recv_sem=recv_sem.at[k],
            device_id=place_of(lax.rem(me + k, count), sec_count),
            device_id_type=MESH,
        )

    def start(k, carry):
        copy(k).start()
        return carry

    def finish(k, carry):
        copy(k).wait()
        return carry

    lax.fori_loop(1, count, start, 0)
    slots[0] = x_ref[...]
    lax.fori_loop(1, count, finish, 0)
    y_ref[...] = jnp.sum(slots[...], axis=0)


def total_power(local_power, count, sec_count):
    beams = local_power.shape[0]
    x = jnp.broadcast_to(local_power[:, None], (beams, 128))
    summed = pl.pallas_call(
        functools.partial(power_kernel, count, sec_count),
        out_shape=jax.ShapeDtypeStruct(x.shape, x.dtype),
        in_specs=[pl.BlockSpec(memory_space=pltpu.VMEM)],
        out_specs=pl.BlockSpec(memory_space=pltpu.VMEM),
        scratch_shapes=[
            pltpu.VMEM((count,) + x.shape, x.dtype),
            pltpu.SemaphoreType.DMA((count,)),
            pltpu.SemaphoreType.DMA((count,)),
        ],
        compiler_params=pltpu.CompilerParams(collective_id=1, has_side_effects=True),
        name="power",
    )(x)
    return summed[:, 0]


def per_device(
    voltages, fir_taps, cor_channels, beam_channels, cor_gain, beam_gain, beam_stations, beam_codes
):
    tap_count, points = fir_taps.shape
    sec_count = lax.axis_size("sec")
    device_count = lax.axis_size("stn") * sec_count
    inputs_here = voltages.shape[1]
    frames = voltages.shape[2] // points
    spectra = frames - tap_count + 1
    slots = 2 * cor_channels.shape[0]
    fits = inputs_here % ROWS == 0 and points % CHUNK == 0 and spectra % 128 == 0
    if not fits or slots != 2 * device_count or slots % 16:
        return plain_device(
            voltages, fir_taps, cor_channels, beam_channels, cor_gain, beam_gain,
            beam_stations, beam_codes,
        )
    channel_of = jnp.concatenate([cor_channels, beam_channels])
    slot_gain = jnp.concatenate([cor_gain, beam_gain])
    table = split_tables(channel_of, points)
    weight_re, weight_im = make_weights(beam_stations, beam_codes, STATIONS)
    outgoing = channelize(voltages, fir_taps, table, slot_gain)
    outgoing = outgoing.reshape(2, device_count, inputs_here, 2 * spectra)
    received = exchange(outgoing, device_count, sec_count)
    received = received.reshape(2, device_count * inputs_here, 2 * spectra)
    cor_data = received[0]
    beam_data = received[1:2]
    raw_beams = form_beams(beam_data, weight_re, weight_im)
    local_power = jnp.sum(raw_beams * raw_beams, axis=(0, 2, 3))
    summed_power = total_power(local_power, device_count, sec_count)
    swapped = jnp.concatenate([cor_data[:, spectra:], -cor_data[:, :spectra]], axis=1)
    vis_re = contract(cor_data, cor_data) / spectra
    vis_im = contract(swapped, cor_data) / spectra
    visibilities = jnp.stack([vis_re, vis_im])[None].astype(jnp.bfloat16)
    beam_power = summed_power / (device_count * raw_beams.shape[2] * raw_beams.shape[3])
    beams = (raw_beams * lax.rsqrt(beam_power + epsilon)[None, :, None, None]).astype(jnp.bfloat16)
    return (visibilities, beams)


def solution(mesh):
    in_specs = (P(None, ("stn", "sec"), None), P(), P(), P(), P(), P(), P(), P())
    out_specs = (P(("stn", "sec"), None, None, None), P(("stn", "sec"), None, None, None))
    return jax.shard_map(
        per_device, mesh=mesh, in_specs=in_specs, out_specs=out_specs, check_vma=False
    )
```
